256 devices in a mesh: pipe: 16 (over x, y), dp: 2 (over z_hi), tensor: 8 (over z_lo, core).
Axes of the slice: x: 4, y: 4, z: 8 (z_hi: 2, z_lo: 4; z = z_hi * 4 + z_lo), core: 2. Of those that a mesh axis runs over, the one named last changes fastest.
Arguments:
- section_states: bfloat16 [16, 2, 256, 8192], P('pipe', 'dp', None, 'tensor'), may hold values from -6 to 6
- key_weight: bfloat16 [16, 8192, 4096], P('pipe', 'dp', 'tensor'), may hold values from -0.0625 to 0.0625
- value_weight: bfloat16 [16, 8192, 4096], P('pipe', 'dp', 'tensor'), may hold values from -0.0625 to 0.0625
- queries: bfloat16 [16, 2, 256, 4096], P('pipe', 'dp', None, 'tensor'), may hold values from -102 to 102
- cotangent: bfloat16 [16, 2, 256, 4096], P('pipe', 'dp', None, 'tensor'), may hold values from -6 to 6
Outputs:
- context: bfloat16 [16, 2, 256, 4096], P('pipe', 'dp', None, 'tensor')
- query_grad: bfloat16 [16, 2, 256, 4096], P('pipe', 'dp', None, 'tensor')
- encoder_grad: bfloat16 [16, 2, 256, 8192], P('pipe', 'dp', None, 'tensor')
The draws below stay inside these ranges and needn't reach their ends.
All inputs are finite; a program needn't handle non-finite values.
Results may differ from the reference program's by a relative error of at most 0.023.
The reference program's roundings to bfloat16 on the way count: a program that leaves them out, or rounds other values in their place, can miss the bound.
Values may be sent and summed in bfloat16 or wider, within the bound.
No kernel may reach another device: no remote copies, remote signals or barrier semaphores. Data moves between devices by JAX's collectives and lax.ppermute only.
A program may use at most 128 MiB of HBM per device.

```python
import jax
import jax.numpy as jnp
from jax import lax

D = 8192
HEADS = 32
HD = 128
ENC = 256
DEC = 256
BATCH = 2
N_PIPE = 16


def draw_queries(key, part):
    key = jax.random.fold_in(key, 11)
    first_key = jax.random.fold_in(key, 0)
    shape = (N_PIPE, BATCH, DEC, HEADS * HD)
    return jnp.clip(jax.random.normal(first_key, shape, jnp.float32), -4.0, 4.0).astype(jnp.bfloat16)


def shard_levels(rng, extent, pieces, least, high):
    gain = 1.0
    for position, blocks in pieces:
        steps = jax.random.uniform(jax.random.fold_in(jax.random.fold_in(rng, 6), position), (blocks,), jnp.float32, least / len(pieces), high / len(pieces))
        gain = gain * jnp.repeat(jnp.exp(steps), extent[position] // blocks).reshape((-1,) + (1,) * (len(extent) - 1 - position))
    return gain


def normal_values(stream_key, dims, spread, reach, pieces=(), dtype=jnp.bfloat16):
    result = spread * jax.random.normal(stream_key, dims, jnp.float32)
    if pieces:
        result = result * shard_levels(stream_key, dims, pieces, -0.22, 0.18)
    return jnp.clip(result, -reach, reach).astype(dtype)


def setup_inputs(seed: int = 0) -> dict:
    keys = jax.random.split(jax.random.key(seed), 6)
    section_states = normal_values(keys[0], (N_PIPE, BATCH, ENC, D), 1.0, 6.0, ((0, 16), (1, 2), (3, 8)))
    key_weight = normal_values(keys[1], (N_PIPE, D, HEADS * HD), D ** -0.5, 0.0625, ((0, 16), (1, 2), (2, 8)))
    value_weight = normal_values(keys[2], (N_PIPE, D, HEADS * HD), D ** -0.5, 0.0625, ((0, 16), (1, 2), (2, 8)))
    queries = draw_queries(jax.random.fold_in(keys[5], 71), 0)
    cotangent = normal_values(keys[4], (N_PIPE, BATCH, DEC, HEADS * HD), 1.0, 6.0, ((0, 16), (1, 2), (3, 8)))
    return dict(section_states=section_states, key_weight=key_weight, value_weight=value_weight, queries=queries, cotangent=cotangent)


def widen(array):
    return lax.optimization_barrier(array.astype(jnp.bfloat16)).astype(jnp.float32)


def section_pass(encoded, key_proj, value_proj, query_rows, grad_rows):
    width = HEADS * HD
    score_scale = HD ** -0.5
    key_rows = jnp.dot(encoded, key_proj, preferred_element_type=jnp.float32)
    value_rows = jnp.dot(encoded, value_proj, preferred_element_type=jnp.float32)
    key_heads = widen(key_rows).reshape(ENC, HEADS, HD)
    value_heads = widen(value_rows).reshape(ENC, HEADS, HD)
    query_heads = query_rows.astype(jnp.float32).reshape(DEC, HEADS, HD)
    grad_heads = grad_rows.astype(jnp.float32).reshape(DEC, HEADS, HD)
    scores = jnp.einsum("qhd,khd->hqk", query_heads, key_heads) * score_scale
    attn_probs = jax.nn.softmax(scores, axis=-1)
    probs_low = widen(attn_probs)
    context = jnp.einsum("hqk,khd->qhd", probs_low, value_heads).reshape(DEC, width)
    dprobs = jnp.einsum("qhd,khd->hqk", grad_heads, value_heads)
    delta = jnp.sum(attn_probs * dprobs, axis=-1, keepdims=True)
    dscores = widen(attn_probs * (dprobs - delta) * score_scale)
    query_grad = jnp.einsum("hqk,khd->qhd", dscores, key_heads).reshape(DEC, width)
    key_grad = jnp.einsum("hqk,qhd->khd", dscores, query_heads).reshape(ENC, width)
    value_grad = jnp.einsum("hqk,qhd->khd", probs_low, grad_heads).reshape(ENC, width)
    key_low = key_grad.astype(jnp.bfloat16)
    value_low = value_grad.astype(jnp.bfloat16)
    section_term = jnp.dot(key_low, key_proj.T, preferred_element_type=jnp.float32)
    section_term = section_term + jnp.dot(value_low, value_proj.T, preferred_element_type=jnp.float32)
    return context.astype(jnp.bfloat16), query_grad.astype(jnp.bfloat16), section_term


def reference(section_states, key_weight, value_weight, queries, cotangent):
    midpoint = N_PIPE // 2
    width = HEADS * HD
    zero_rows = jnp.zeros((BATCH, DEC, width), jnp.bfloat16)
    contexts = []
    query_grads = []
    totals = [jnp.zeros((ENC, D), jnp.float32) for member in range(BATCH)]
    for section in range(N_PIPE):
        if section < midpoint:
            contexts.append(zero_rows)
            query_grads.append(zero_rows)
            continue
        section_ctx = []
        section_qg = []
        for member in range(BATCH):
            ctx, qgrad, term = section_pass(section_states[midpoint - 1, member], key_weight[section], value_weight[section], queries[section, member], cotangent[section, member])
            section_ctx.append(ctx)
            section_qg.append(qgrad)
            totals[member] = totals[member] + term
        contexts.append(jnp.stack(section_ctx))
        query_grads.append(jnp.stack(section_qg))
    summed = jnp.stack(totals).astype(jnp.bfloat16)
    blank = jnp.zeros((BATCH, ENC, D), jnp.bfloat16)
    grads = [summed if section == midpoint - 1 else blank for section in range(N_PIPE)]
    return jnp.stack(contexts), jnp.stack(query_grads), jnp.stack(grads)
```

```python
import jax
import jax.numpy as jnp
from jax import lax
from jax.sharding import PartitionSpec as P

HD = 128
AXES = ("pipe", "dp", "tensor")
F32 = jnp.float32
BF16 = jnp.bfloat16


def body(section_states, key_weight, value_weight, queries, cotangent):
    sections = lax.axis_size("pipe")
    replicas = lax.axis_size("dp")
    lanes = lax.axis_size("tensor")
    first = sections // 2
    count = sections - first
    root = first - 1
    section = lax.axis_index("pipe")
    replica = lax.axis_index("dp")
    lane = lax.axis_index("tensor")
    core = lane % 2
    chip = lane // 2
    chips = lanes // 2
    decoder = section >= first

    def place(s, d, t):
        return (s * replicas + d) * lanes + t

    everyone = [(k, d, t) for k in range(count) for d in range(replicas) for t in range(lanes)]

    def send(array, move):
        pairs = []
        for k, d, t in everyone:
            a, b, c = move(k, d, t)
            pairs.append((place(first + k, d, t), place(first + a, b, c)))
        return lax.ppermute(array, AXES, pairs)

    def swap_core(array):
        return send(array, lambda k, d, t: (k, d, t ^ 1))

    def swap_replica(array):
        return send(array, lambda k, d, t: (k, 1 - d, t))

    half = lanes // 2
    piece = section_states[0, 0]
    tokens, block = piece.shape
    rows = tokens // count

    local = key_weight.shape[2]

    def split(weight):
        parts = weight[0].reshape(2, 2, block, local)
        mine = lax.dynamic_index_in_dim(parts, core, 1, keepdims=False).reshape(2 * block, local)
        other = lax.dynamic_index_in_dim(parts, 1 - core, 1, keepdims=False).reshape(
            2 * block, local
        )
        return mine, other

    key_mine, key_other = split(key_weight)
    value_mine, value_other = split(value_weight)
    key_far = swap_core(key_other)
    value_far = swap_core(value_other)
    back = jnp.concatenate([key_mine, value_mine, key_far, value_far], axis=1)

    got = None
    for k in range(count):
        pairs = [
            (place(root, b, half * p + j), place(first + k, p, half * b + j))
            for b in range(replicas)
            for p in range(replicas)
            for j in range(half)
        ]
        part = lax.ppermute(piece[k * rows : (k + 1) * rows], AXES, pairs)
        got = part if got is None else got + part
    held = [got] + [
        send(got, lambda k, d, t, n=n: (k, d, t ^ (2 * n))) for n in range(1, chips)
    ]
    held = jnp.stack(held)

    def pick(array, owner):
        return lax.dynamic_index_in_dim(array, chip ^ owner, 0, keepdims=False)

    chunk = jnp.stack(
        [
            jnp.concatenate([pick(held, 2 * b), pick(held, 2 * b + 1)], axis=1)
            for b in (replica, 1 - replica)
        ]
    )
    chunks = [chunk] + [
        send(chunk, lambda k, d, t, m=m: (k ^ m, d, t)) for m in range(1, count)
    ]
    near = jnp.stack(chunks, axis=1).reshape(replicas * tokens, 2 * block)
    far = swap_core(near)

    def project(mine, other):
        out = jnp.dot(near, mine, preferred_element_type=F32)
        return out + jnp.dot(far, other, preferred_element_type=F32)

    key_part = project(key_mine, key_other)
    key_sum = key_part[:tokens] + swap_replica(key_part[tokens:])
    value_part = project(value_mine, value_other)
    value_sum = value_part[:tokens] + swap_replica(value_part[tokens:].astype(BF16)).astype(F32)

    heads = local // HD
    dec_len = queries.shape[2]
    keys = key_sum.astype(BF16).reshape(tokens, heads, HD)
    values = value_sum.astype(BF16).reshape(tokens, heads, HD)
    query = queries[0, 0].reshape(dec_len, heads, HD)
    grad = cotangent[0, 0].reshape(dec_len, heads, HD)
    scale = HD ** (-0.5)
    scores = jnp.einsum("qhd,khd->hqk", query, keys, preferred_element_type=F32) * scale
    top = jnp.max(scores, axis=-1, keepdims=True)
    weights = jnp.exp(scores - top)
    probs = weights / jnp.sum(weights, axis=-1, keepdims=True)
    low = probs.astype(BF16)
    value_grad = (
        jnp.einsum("hqk,qhd->khd", low, grad, preferred_element_type=F32)
        .reshape(tokens, local)
        .astype(BF16)
    )
    value_grad_far = swap_replica(value_grad)
    dprobs = jnp.einsum("qhd,khd->hqk", grad, values, preferred_element_type=F32)
    delta = jnp.sum(probs * dprobs, axis=-1, keepdims=True)
    dscores = (probs * (dprobs - delta) * scale).astype(BF16)
    key_grad = (
        jnp.einsum("hqk,qhd->khd", dscores, query, preferred_element_type=F32)
        .reshape(tokens, local)
        .astype(BF16)
    )
    key_grad_far = swap_replica(key_grad)
    context = jnp.einsum("hqk,khd->qhd", low, values, preferred_element_type=F32)
    context = context.reshape(dec_len, local)
    query_grad = jnp.einsum("hqk,khd->qhd", dscores, keys, preferred_element_type=F32)
    query_grad = query_grad.reshape(dec_len, local)

    here = jnp.concatenate([key_grad, value_grad], axis=1)
    there = jnp.concatenate([key_grad_far, value_grad_far], axis=1)
    grads = jnp.concatenate(
        [
            jnp.concatenate([here, swap_core(here)], axis=1),
            jnp.concatenate([there, swap_core(there)], axis=1),
        ],
        axis=0,
    )
    term = lax.dot_general(
        grads, back, (((1,), (1,)), ((), ())), preferred_element_type=F32
    )
    term = term.reshape(replicas, count, rows, 2 * block)
    total = term[:, 0]
    term_low = term.astype(BF16)
    for m in range(1, count):
        total = total + send(term_low[:, m], lambda k, d, t, m=m: (k ^ m, d, t)).astype(F32)
    total = total.reshape(replicas, rows, 2, block)

    def owned(array, owner):
        which = (owner // 2) ^ replica
        one = lax.dynamic_index_in_dim(array, which, 0, keepdims=False)
        return lax.dynamic_index_in_dim(one, owner % 2, 1, keepdims=False)

    summed = owned(total, chip)
    for n in range(1, chips):
        away = owned(total, chip ^ n).astype(BF16)
        summed = summed + send(away, lambda k, d, t, n=n: (k, d, t ^ (2 * n))).astype(F32)
    summed = summed.astype(BF16)
    out = []
    for k in range(count):
        pairs = [
            (place(first + k, p, half * b + j), place(root, b, half * p + j))
            for b in range(replicas)
            for p in range(replicas)
            for j in range(half)
        ]
        out.append(lax.ppermute(summed, AXES, pairs))
    encoder_grad = jnp.concatenate(out, axis=0)
    encoder_grad = jnp.where(section == root, encoder_grad, jnp.zeros_like(encoder_grad))
    context = jnp.where(decoder, context, 0.0).astype(BF16)
    query_grad = jnp.where(decoder, query_grad, 0.0).astype(BF16)
    return context[None, None], query_grad[None, None], encoder_grad[None, None]


def solution(mesh):
    wide = P("pipe", "dp", None, "tensor")
    tall = P("pipe", "dp", "tensor")
    return jax.shard_map(
        body,
        mesh=mesh,
        in_specs=(wide, tall, tall, wide, wide),
        out_specs=(wide, wide, wide),
        check_vma=False,
    )
```

```python
import functools

import jax
import jax.numpy as jnp
from jax import lax
from jax.experimental import pallas as pl
from jax.experimental.pallas import tpu as pltpu
from jax.sharding import PartitionSpec as P

HD = 128
AXES = ("pipe", "dp", "tensor")
F32 = jnp.float32
BF16 = jnp.bfloat16
SCALE = HD ** (-0.5)
VMEM = 20 * 1024 * 1024
VMEM_BACK = 48 * 1024 * 1024
BACK_COST = 8 << 20
NT = (((1,), (1,)), ((), ()))
TN = (((0,), (0,)), ((), ()))


def params():
    return pltpu.CompilerParams(vmem_limit_bytes=VMEM)


def like(shape, dtype):
    return jax.ShapeDtypeStruct(shape, dtype)


def dot(a, b, dims=(((1,), (0,)), ((), ()))):
    return lax.dot_general(a, b, dims, preferred_element_type=F32)


def cost(moved=1):
    return pl.CostEstimate(flops=1, bytes_accessed=moved, transcendentals=0)


def whole(count):
    return [pl.BlockSpec(memory_space=pltpu.VMEM)] * count


def scalar():
    return [pl.BlockSpec(memory_space=pltpu.SMEM)]


def rows_of(weight, index, size):
    return weight[pl.ds(pl.multiple_of(index * size, size), size), :]


def product_near(core, near, key_weight, value_weight, block):
    count, sequences, rows, width = near.shape
    tokens = count * sequences * rows
    cols = key_weight.shape[1]
    step = block // 2

    def kernel(core_ref, x_ref, wk, wv, ok, ov):
        x = x_ref[...].reshape(tokens, step)
        shape = (count, sequences, rows, cols)

        @pl.when(pl.program_id(0) == 0)
        def _():
            ok[...] = dot(x, wk[...]).reshape(shape)
            ov[...] = dot(x, wv[...]).reshape(shape)

        @pl.when(pl.program_id(0) > 0)
        def _():
            ok[...] += dot(x, wk[...]).reshape(shape)
            ov[...] += dot(x, wv[...]).reshape(shape)

    def place(i, c):
        return ((i // 2 * 2 + c[0]) * 2 + i % 2, 0)

    return pl.pallas_call(
        kernel,
        grid_spec=pltpu.PrefetchScalarGridSpec(
            num_scalar_prefetch=1,
            grid=(width // step,),
            in_specs=[
                pl.BlockSpec((count, sequences, rows, step), lambda i, c: (0, 0, 0, i)),
                pl.BlockSpec((step, cols), place),
                pl.BlockSpec((step, cols), place),
            ],
            out_specs=[
                pl.BlockSpec((count, sequences, rows, cols), lambda i, c: (0, 0, 0, 0))
            ]
            * 2,
        ),
        out_shape=[like((count, sequences, rows, cols), F32)] * 2,
        cost_estimate=cost(),
        compiler_params=params(),
    )(core, near, key_weight, value_weight)


def product_far(core, far, weights, parts, block, which, sent):
    count, sequences, rows, width = far.shape
    tokens = count * rows
    cols = weights[0].shape[1]
    many = len(weights)

    def kernel(core_ref, x_ref, *refs):
        ws, ps, outs = (refs[n * many : (n + 1) * many] for n in range(3))
        c = 1 - core_ref[0]
        for w, p, out in zip(ws, ps, outs):
            total = p[:, which].reshape(tokens, cols)
            for j in range(2):
                x = x_ref[:, which, :, j * block : (j + 1) * block].reshape(tokens, block)
                total = total + dot(x, rows_of(w, 2 * j + c, block))
            out[...] = total.astype(out.dtype)

    return pl.pallas_call(
        kernel,
        in_specs=scalar() + whole(1 + 2 * many),
        out_specs=whole(many),
        out_shape=[like((tokens, cols), t) for t in sent],
        cost_estimate=cost(),
        compiler_params=params(),
    )(core, far, *weights, *parts)


def other_rows(core, key_weight, value_weight, block, after):
    height, cols = key_weight.shape
    step = block // 2

    def kernel(core_ref, wk, wv, after_ref, out):
        out[0] = wk[...]
        out[1] = wv[...]

    def place(i, c):
        return ((i // 2 * 2 + 1 - c[0]) * 2 + i % 2, 0)

    return pl.pallas_call(
        kernel,
        grid_spec=pltpu.PrefetchScalarGridSpec(
            num_scalar_prefetch=1,
            grid=(4,),
            in_specs=[pl.BlockSpec((step, cols), place)] * 2
            + [pl.BlockSpec(memory_space=pl.ANY)],
            out_specs=pl.BlockSpec((2, step, cols), lambda i, c: (0, i, 0)),
        ),
        out_shape=like((2, height // 2, cols), BF16),
        cost_estimate=cost(),
        compiler_params=params(),
    )(core, key_weight, value_weight, after)


def attend(key_own, key_in, value_own, value_in, query, grad):
    tokens, local = key_own.shape
    dec = query.shape[0]
    heads = local // HD

    def kernel(ka, kb, va, vb, q, g, keys, values, low, dscores, grads):
        for h in range(heads):
            at = slice(h * HD, (h + 1) * HD)
            k = (ka[:, at] + kb[:, at]).astype(BF16)
            v = (va[:, at] + vb[:, at].astype(F32)).astype(BF16)
            keys[:, at] = k
            values[:, at] = v
            scores = dot(q[:, at], k, NT) * SCALE
            top = jnp.max(scores, axis=-1, keepdims=True)
            e = jnp.exp(scores - top)
            p = e / jnp.sum(e, axis=-1, keepdims=True)
            rounded = p.astype(BF16)
            low[h] = rounded
            dprobs = dot(g[:, at], v, NT)
            delta = jnp.sum(p * dprobs, axis=-1, keepdims=True)
            ds = (p * (dprobs - delta) * SCALE).astype(BF16)
            dscores[h] = ds
            grads[:, at] = dot(ds, q[:, at], TN).astype(BF16)
            start = local + h * HD
            grads[:, start : start + HD] = dot(rounded, g[:, at], TN).astype(BF16)

    return pl.pallas_call(
        kernel,
        in_specs=whole(6),
        out_specs=whole(5),
        out_shape=[
            like((tokens, local), BF16),
            like((tokens, local), BF16),
            like((heads, dec, tokens), BF16),
            like((heads, dec, tokens), BF16),
            like((tokens, 2 * local), BF16),
        ],
        cost_estimate=cost(),
        compiler_params=params(),
    )(key_own, key_in, value_own, value_in, query, grad)


def attend_out(keep, low, values, dscores, keys):
    tokens, local = values.shape
    heads, dec = low.shape[:2]

    def kernel(keep_ref, p, v, ds, k, context, query_grad):
        on = keep_ref[0] > 0
        for h in range(heads):
            at = slice(h * HD, (h + 1) * HD)
            context[:, at] = jnp.where(on, dot(p[h], v[:, at]), 0.0).astype(BF16)
            query_grad[:, at] = jnp.where(on, dot(ds[h], k[:, at]), 0.0).astype(BF16)

    return pl.pallas_call(
        kernel,
        in_specs=scalar() + whole(4),
        out_specs=whole(2),
        out_shape=[like((dec, local), BF16)] * 2,
        cost_estimate=cost(),
        compiler_params=params(),
    )(keep, low, values, dscores, keys)


def back_product_near(core, mine, others, key_weight, value_weight, weights_far, block, count):
    tokens = mine[0].shape[0]
    cols = key_weight.shape[1]
    width = 2 * block
    step = block // 2
    rows = tokens // count
    split = len(mine), len(mine) + len(others)

    def kernel(core_ref, *refs):
        wk, wv, far, low = refs[split[1] :]
        c = core_ref[0]

        def pair(arrays):
            if len(arrays) == 1:
                return arrays[0][:, :cols], arrays[0][:, cols:]
            return arrays[0][...], arrays[1][...]

        (kg, vg), (kh, vh) = pair(refs[: split[0]]), pair(refs[split[0] : split[1]])
        for i in range(width // step):
            at = (i // 2 * 2 + c) * 2 + i % 2
            total = dot(kg, rows_of(wk, at, step), NT)
            total += dot(vg, rows_of(wv, at, step), NT)
            total += dot(kh, far[0, i * step : (i + 1) * step, :], NT)
            total += dot(vh, far[1, i * step : (i + 1) * step, :], NT)
            low[:, :, i * step : (i + 1) * step] = total.reshape(count, rows, step).astype(BF16)

    return pl.pallas_call(
        kernel,
        in_specs=scalar() + whole(split[1] + 3),
        out_specs=whole(1)[0],
        out_shape=like((count, rows, width), BF16),
        cost_estimate=cost(),
        compiler_params=params(),
    )(core, *mine, *others, key_weight, value_weight, weights_far)


def back_product(core, mine, others, key_weight, value_weight, weights_far, block, count):
    tokens = mine[0].shape[0]
    cols = key_weight.shape[1]
    width = 2 * block
    step = block // 2
    rows = tokens // count
    split = len(mine), len(mine) + len(others)

    def kernel(core_ref, *refs):
        wk, wv, fk, fv, low = refs[split[1] :]

        def pair(arrays):
            if len(arrays) == 1:
                return arrays[0][:, :cols], arrays[0][:, cols:]
            return arrays[0][...], arrays[1][...]

        (kg, vg), (kh, vh) = pair(refs[: split[0]]), pair(refs[split[0] : split[1]])
        total = dot(kg, wk[...], NT)
        total += dot(vg, wv[...], NT)
        total += dot(kh, fk[0], NT)
        total += dot(vh, fv[0], NT)
        low[...] = total.reshape(count, rows, step).astype(BF16)

    def place(i, c):
        return ((i // 2 * 2 + c[0]) * 2 + i % 2, 0)

    return pl.pallas_call(
        kernel,
        grid_spec=pltpu.PrefetchScalarGridSpec(
            num_scalar_prefetch=1,
            grid=(width // step,),
            in_specs=[pl.BlockSpec(a.shape, lambda i, c: (0, 0)) for a in (*mine, *others)]
            + [pl.BlockSpec((step, cols), place)] * 2
            + [
                pl.BlockSpec((1, step, cols), lambda i, c: (0, i, 0)),
                pl.BlockSpec((1, step, cols), lambda i, c: (1, i, 0)),
            ],
            out_specs=pl.BlockSpec((count, rows, step), lambda i, c: (0, 0, i)),
        ),
        out_shape=like((count, rows, width), BF16),
        cost_estimate=cost(BACK_COST),
        compiler_params=pltpu.CompilerParams(vmem_limit_bytes=VMEM_BACK),
    )(core, *mine, *others, key_weight, value_weight, weights_far, weights_far)


def body(section_states, key_weight, value_weight, queries, cotangent):
    sections = lax.axis_size("pipe")
    replicas = lax.axis_size("dp")
    lanes = lax.axis_size("tensor")
    first = sections // 2
    count = sections - first
    root = first - 1
    section = lax.axis_index("pipe")
    replica = lax.axis_index("dp")
    lane = lax.axis_index("tensor")
    core = lane % 2
    chip = lane // 2
    chips = lanes // 2
    decoder = section >= first
    half = lanes // 2

    def place(s, d, t):
        return (s * replicas + d) * lanes + t

    everyone = [(k, d, t) for k in range(count) for d in range(replicas) for t in range(lanes)]

    def send(array, move):
        pairs = []
        for k, d, t in everyone:
            a, b, c = move(k, d, t)
            pairs.append((place(first + k, d, t), place(first + a, b, c)))
        return lax.ppermute(array, AXES, pairs)

    def swap_core(array):
        return send(array, lambda k, d, t: (k, d, t ^ 1))

    def swap_replica(array):
        return send(array, lambda k, d, t: (k, 1 - d, t))

    def beside(k, d, t):
        return place((k + count // 2) % count, d, t)

    def lend(array):
        pairs = [(place(first + k, d, t), beside(k, d, t)) for k, d, t in everyone]
        return lax.ppermute(array, AXES, pairs)

    def swap_replica_lent(array):
        pairs = [(beside(k, d, t), place(first + k, 1 - d, t)) for k, d, t in everyone]
        return lax.ppermute(array, AXES, pairs)

    groups = [list(range(first)), list(range(first, sections))]

    def exchange(array):
        return lax.all_to_all(array, "pipe", 0, 0, axis_index_groups=groups)

    def cross(k, d, t, n):
        owner = 2 * d + (t % half) // 2
        return (k, t // half, 2 * (owner ^ n) + t % 2)

    def cross_back(k, d, t, n):
        owner = (t // 2) ^ n
        return (k, owner // 2, half * d + 2 * (owner % 2) + t % 2)

    piece = section_states[0, 0]
    key_weight, value_weight = key_weight[0], value_weight[0]
    tokens, block = piece.shape
    rows = tokens // count
    local = key_weight.shape[1]
    core_index = core.astype(jnp.int32).reshape(1)

    got = None
    for k in range(count):
        pairs = [
            (place(root, d, t), place(first + k, d, t))
            for d in range(replicas)
            for t in range(lanes)
        ]
        part = lax.ppermute(piece[k * rows : (k + 1) * rows], AXES, pairs)
        got = part if got is None else got + part
    held = jnp.stack(
        [send(got, functools.partial(cross, n=n)) for n in range(chips)]
    )

    def pick(owner):
        return lax.dynamic_index_in_dim(held, chip ^ owner, 0, keepdims=False)

    chunk = jnp.stack(
        [
            jnp.concatenate([pick(2 * b), pick(2 * b + 1)], axis=1)
            for b in (replica, 1 - replica)
        ]
    )
    near = exchange(jnp.broadcast_to(chunk[None], (count,) + chunk.shape))
    far = swap_core(near)
    key_part, value_part = product_near(core_index, near, key_weight, value_weight, block)
    weights = [key_weight, value_weight]
    far_product = functools.partial(product_far, core_index, far, weights)
    key_out, value_out = far_product([key_part, value_part], block, 1, [F32, BF16])
    key_in = swap_replica(key_out)
    lent = lend(value_out)
    value_in = swap_replica_lent(lent)
    key_part, value_part, lent = lax.optimization_barrier((key_part, value_part, lent))
    key_own, value_own = far_product([key_part, value_part], block, 0, [F32, F32])

    query, grad = queries[0, 0], cotangent[0, 0]
    keys, values, low, dscores, grads = attend(
        key_own, key_in, value_own, value_in, query, grad
    )
    grads_in = swap_replica(grads)
    keep = decoder.astype(jnp.int32).reshape(1)
    context, query_grad = attend_out(keep, low, values, dscores, keys)

    weights_far = swap_core(other_rows(core_index, key_weight, value_weight, block, grads))

    def reduce(term):
        return jnp.sum(exchange(term).astype(F32), axis=0)

    own_total = reduce(
        back_product_near(
            core_index, [grads], [swap_core(grads)], *weights, weights_far, block, count
        )
    )
    other_term = back_product(
        core_index, [grads_in], [swap_core(grads_in)], *weights, weights_far, block, count
    )
    other_term, own_total = lax.optimization_barrier((other_term, own_total))
    other_total = reduce(other_term)
    total = jnp.stack([own_total, other_total])
    total = total.reshape(replicas, rows, 2, block)

    def owned(owner):
        one = lax.dynamic_index_in_dim(total, (owner // 2) ^ replica, 0, keepdims=False)
        return lax.dynamic_index_in_dim(one, owner % 2, 1, keepdims=False)

    summed = None
    for n in reversed(range(chips)):
        part = send(owned(chip ^ n).astype(BF16), functools.partial(cross_back, n=n))
        part = part.astype(F32)
        summed = part if summed is None else summed + part
    summed = summed.astype(BF16)
    out = []
    for k in range(count):
        pairs = [
            (place(first + k, d, t), place(root, d, t))
            for d in range(replicas)
            for t in range(lanes)
        ]
        out.append(lax.ppermute(summed, AXES, pairs))
    out = lax.optimization_barrier(out)
    encoder_grad = jnp.concatenate(out, axis=0)
    encoder_grad = jnp.where(section == root, encoder_grad, jnp.zeros_like(encoder_grad))
    return context[None, None], query_grad[None, None], encoder_grad[None, None]


def solution(mesh):
    wide = P("pipe", "dp", None, "tensor")
    tall = P("pipe", "dp", "tensor")
    return jax.shard_map(
        body,
        mesh=mesh,
        in_specs=(wide, tall, tall, wide, wide),
        out_specs=(wide, wide, wide),
        check_vma=False,
    )
```

```python
import functools

import jax
import jax.numpy as jnp
from jax import lax
from jax.experimental import pallas as pl
from jax.experimental.pallas import tpu as pltpu
from jax.sharding import PartitionSpec as P

HD = 128
AXES = ("pipe", "dp", "tensor")
F32 = jnp.float32
BF16 = jnp.bfloat16
SCALE = HD ** (-0.5)
VMEM = 20 * 1024 * 1024
VMEM_BACK = 48 * 1024 * 1024
NT = (((1,), (1,)), ((), ()))
TN = (((0,), (0,)), ((), ()))


def params():
    return pltpu.CompilerParams(vmem_limit_bytes=VMEM)


def like(shape, dtype):
    return jax.ShapeDtypeStruct(shape, dtype)


def dot(a, b, dims=(((1,), (0,)), ((), ()))):
    return lax.dot_general(a, b, dims, preferred_element_type=F32)


def cost():
    return pl.CostEstimate(flops=1, bytes_accessed=1, transcendentals=0)


def whole(count):
    return [pl.BlockSpec(memory_space=pltpu.VMEM)] * count


def scalar():
    return [pl.BlockSpec(memory_space=pltpu.SMEM)]


def rows_of(weight, index, size):
    return weight[pl.ds(pl.multiple_of(index * size, size), size), :]


def product_near(near, weights, block):
    count, rows, width = near.shape
    tokens = count * rows
    cols = weights[0].shape[1]
    many = len(weights)

    def kernel(x_ref, *refs):
        x = x_ref[...].reshape(tokens, block)
        first = pl.program_id(0) == 0
        for w, out in zip(refs[:many], refs[many:]):

            @pl.when(first)
            def _():
                out[...] = dot(x, w[...])

            @pl.when(jnp.logical_not(first))
            def _():
                out[...] += dot(x, w[...])

    return pl.pallas_call(
        kernel,
        grid=(width // block,),
        in_specs=[pl.BlockSpec((count, rows, block), lambda i: (0, 0, i))]
        + [pl.BlockSpec((block, cols), lambda i: (i, 0))] * many,
        out_specs=[pl.BlockSpec((tokens, cols), lambda i: (0, 0))] * many,
        out_shape=[like((tokens, cols), F32)] * many,
        cost_estimate=cost(),
        compiler_params=params(),
    )(near, *weights)


def product_far(same, far, weights, parts):
    count, rows, width = far.shape
    tokens = count * rows
    cols = weights[0].shape[1]

    def kernel(same_ref, x_ref, wk, wv, pk, pv, key_out, value_out, key_own, value_own):
        same_here = same_ref[0] > 0
        x = x_ref[...].reshape(tokens, width)
        for w, p, out, own in ((wk, pk, key_out, key_own), (wv, pv, value_out, value_own)):
            total = dot(x, w[...])
            part = p[...]
            out[...] = jnp.where(same_here, total, part).astype(out.dtype)
            own[...] = jnp.where(same_here, part, total)

    return pl.pallas_call(
        kernel,
        in_specs=scalar() + whole(5),
        out_specs=whole(4),
        out_shape=[like((tokens, cols), t) for t in (F32, BF16, F32, F32)],
        cost_estimate=cost(),
        compiler_params=params(),
    )(same, far, *weights, *parts)


def other_rows(core, key_weight, value_weight, block, after):
    height, cols = key_weight.shape
    step = block // 2

    def kernel(core_ref, wk, wv, after_ref, out):
        out[0] = wk[...]
        out[1] = wv[...]

    def place(i, c):
        return ((i // 2 * 2 + 1 - c[0]) * 2 + i % 2, 0)

    return pl.pallas_call(
        kernel,
        grid_spec=pltpu.PrefetchScalarGridSpec(
            num_scalar_prefetch=1,
            grid=(4,),
            in_specs=[pl.BlockSpec((step, cols), place)] * 2
            + [pl.BlockSpec(memory_space=pl.ANY)],
            out_specs=pl.BlockSpec((2, step, cols), lambda i, c: (0, i, 0)),
        ),
        out_shape=like((2, height // 2, cols), BF16),
        cost_estimate=cost(),
        compiler_params=params(),
    )(core, key_weight, value_weight, after)


def attend(key_own, key_in, value_own, value_in, query, grad):
    tokens, local = key_own.shape
    dec = query.shape[0]
    heads = local // HD

    def kernel(ka, kb, va, vb, q, g, keys, values, low, dscores, grads):
        for h in range(heads):
            at = slice(h * HD, (h + 1) * HD)
            k = (ka[:, at] + kb[:, at]).astype(BF16)
            v = (va[:, at] + vb[:, at].astype(F32)).astype(BF16)
            keys[:, at] = k
            values[:, at] = v
            scores = dot(q[:, at], k, NT) * SCALE
            top = jnp.max(scores, axis=-1, keepdims=True)
            e = jnp.exp(scores - top)
            p = e / jnp.sum(e, axis=-1, keepdims=True)
            rounded = p.astype(BF16)
            low[h] = rounded
            dprobs = dot(g[:, at], v, NT)
            delta = jnp.sum(p * dprobs, axis=-1, keepdims=True)
            ds = (p * (dprobs - delta) * SCALE).astype(BF16)
            dscores[h] = ds
            grads[:, at] = dot(ds, q[:, at], TN).astype(BF16)
            start = local + h * HD
            grads[:, start : start + HD] = dot(rounded, g[:, at], TN).astype(BF16)

    return pl.pallas_call(
        kernel,
        in_specs=whole(6),
        out_specs=whole(5),
        out_shape=[
            like((tokens, local), BF16),
            like((tokens, local), BF16),
            like((heads, dec, tokens), BF16),
            like((heads, dec, tokens), BF16),
            like((tokens, 2 * local), BF16),
        ],
        cost_estimate=cost(),
        compiler_params=params(),
    )(key_own, key_in, value_own, value_in, query, grad)


def attend_out(keep, low, values, dscores, keys):
    tokens, local = values.shape
    heads, dec = low.shape[:2]

    def kernel(keep_ref, p, v, ds, k, context, query_grad):
        on = keep_ref[0] > 0
        for h in range(heads):
            at = slice(h * HD, (h + 1) * HD)
            context[:, at] = jnp.where(on, dot(p[h], v[:, at]), 0.0).astype(BF16)
            query_grad[:, at] = jnp.where(on, dot(ds[h], k[:, at]), 0.0).astype(BF16)

    return pl.pallas_call(
        kernel,
        in_specs=scalar() + whole(4),
        out_specs=whole(2),
        out_shape=[like((dec, local), BF16)] * 2,
        cost_estimate=cost(),
        compiler_params=params(),
    )(keep, low, values, dscores, keys)


def back_product_near(core, mine, others, key_weight, value_weight, weights_far, block, count):
    tokens = mine.shape[0]
    cols = key_weight.shape[1]
    width = 2 * block
    step = block // 2
    rows = tokens // count

    def kernel(core_ref, g, h, wk, wv, far, out, low, sems):
        c = core_ref[0]
        copies = []
        for i in range(width // step):
            at = (i // 2 * 2 + c) * 2 + i % 2
            total = dot(g[:, :cols], rows_of(wk, at, step), NT)
            total += dot(g[:, cols:], rows_of(wv, at, step), NT)
            total += dot(h[:, :cols], far[0, i * step : (i + 1) * step, :], NT)
            total += dot(h[:, cols:], far[1, i * step : (i + 1) * step, :], NT)
            low[i] = total.reshape(count, rows, step).astype(BF16)
            copy = pltpu.make_async_copy(
                low.at[i], out.at[:, :, pl.ds(i * step, step)], sems.at[i]
            )
            copy.start()
            copies.append(copy)
        for copy in copies:
            copy.wait()

    return pl.pallas_call(
        kernel,
        in_specs=scalar() + whole(5),
        out_specs=pl.BlockSpec(memory_space=pltpu.HBM),
        out_shape=like((count, rows, width), BF16),
        scratch_shapes=[
            pltpu.VMEM((width // step, count, rows, step), BF16),
            pltpu.SemaphoreType.DMA((width // step,)),
        ],
        cost_estimate=cost(),
        compiler_params=params(),
    )(core, mine, others, key_weight, value_weight, weights_far)


def back_product(core, mine, others, key_weight, value_weight, weights_far, block, count):
    tokens = mine.shape[0]
    cols = key_weight.shape[1]
    width = 2 * block
    step = block // 2
    steps = width // step
    rows = tokens // count

    def kernel(core_ref, g, h, wk, wv, far, out, held, low, in_sems, out_sems):
        c = core_ref[0]
        loads = []
        for i in range(steps):
            at = pl.ds(pl.multiple_of(((i // 2 * 2 + c) * 2 + i % 2) * step, step), step)
            sources = [wk.at[at], wv.at[at]]
            sources += [far.at[n, pl.ds(i * step, step)] for n in range(2)]
            loads.append(
                [
                    pltpu.make_async_copy(source, held.at[i, n], in_sems.at[i, n])
                    for n, source in enumerate(sources)
                ]
            )
        for group in loads:
            for load in group:
                load.start()
        stores = []
        for i in range(steps):
            total = None
            for n, a in enumerate((g, g, h, h)):
                loads[i][n].wait()
                term = dot(a[:, n % 2 * cols : (n % 2 + 1) * cols], held[i, n], NT)
                total = term if total is None else total + term
            low[i] = total.reshape(count, rows, step).astype(BF16)
            store = pltpu.make_async_copy(
                low.at[i], out.at[:, :, pl.ds(i * step, step)], out_sems.at[i]
            )
            store.start()
            stores.append(store)
        for store in stores:
            store.wait()

    return pl.pallas_call(
        kernel,
        in_specs=scalar() + whole(2) + [pl.BlockSpec(memory_space=pl.ANY)] * 3,
        out_specs=pl.BlockSpec(memory_space=pl.ANY),
        out_shape=like((count, rows, width), BF16),
        scratch_shapes=[
            pltpu.VMEM((steps, 4, step, cols), BF16),
            pltpu.VMEM((steps, count, rows, step), BF16),
            pltpu.SemaphoreType.DMA((steps, 4)),
            pltpu.SemaphoreType.DMA((steps,)),
        ],
        cost_estimate=cost(),
        compiler_params=pltpu.CompilerParams(vmem_limit_bytes=VMEM_BACK),
    )(core, mine, others, key_weight, value_weight, weights_far)


def body(section_states, key_weight, value_weight, queries, cotangent):
    sections = lax.axis_size("pipe")
    replicas = lax.axis_size("dp")
    lanes = lax.axis_size("tensor")
    first = sections // 2
    count = sections - first
    root = first - 1
    section = lax.axis_index("pipe")
    replica = lax.axis_index("dp")
    lane = lax.axis_index("tensor")
    core = lane % 2
    chip = lane // 2
    chips = lanes // 2
    decoder = section >= first
    half = lanes // 2

    def place(s, d, t):
        return (s * replicas + d) * lanes + t

    everyone = [(k, d, t) for k in range(count) for d in range(replicas) for t in range(lanes)]

    def send(array, move):
        pairs = []
        for k, d, t in everyone:
            a, b, c = move(k, d, t)
            pairs.append((place(first + k, d, t), place(first + a, b, c)))
        return lax.ppermute(array, AXES, pairs)

    def swap_core(array):
        return send(array, lambda k, d, t: (k, d, t ^ 1))

    def swap_replica(array):
        return send(array, lambda k, d, t: (k, 1 - d, t))

    def beside(k, d, t):
        return place((k + count // 2) % count, d, t)

    def lend(array):
        pairs = [(place(first + k, d, t), beside(k, d, t)) for k, d, t in everyone]
        return lax.ppermute(array, AXES, pairs)

    def swap_replica_lent(array):
        pairs = [(beside(k, d, t), place(first + k, 1 - d, t)) for k, d, t in everyone]
        return lax.ppermute(array, AXES, pairs)

    groups = [list(range(first)), list(range(first, sections))]

    def exchange(array):
        return lax.all_to_all(array, "pipe", 0, 0, axis_index_groups=groups)

    def cross(k, d, t, n):
        over = 2 * (t % 2) + (n ^ (t % half) // 2)
        return (k, t // half, 2 * over + d)

    def cross_back(k, d, t, n):
        owner = (t // 2) ^ n
        return (k, owner // 2, half * d + 2 * (owner % 2) + t % 2)

    def in_order(mine, others):
        return jnp.where(core == 0, mine, others), jnp.where(core == 0, others, mine)

    piece = section_states[0, 0]
    key_weight, value_weight = key_weight[0], value_weight[0]
    tokens, block = piece.shape
    rows = tokens // count
    local = key_weight.shape[1]
    core_index = core.astype(jnp.int32).reshape(1)

    got = None
    for k in range(count):
        pairs = [
            (place(root, d, t), place(first + k, d, t))
            for d in range(replicas)
            for t in range(lanes)
        ]
        part = lax.ppermute(piece[k * rows : (k + 1) * rows], AXES, pairs)
        got = part if got is None else got + part
    both = jnp.concatenate(in_order(got, swap_core(got)), axis=1)
    held = [send(both, functools.partial(cross, n=n)) for n in range(2)]
    even = chip % 2 == 0
    chunk = jnp.concatenate(
        [jnp.where(even, held[0], held[1]), jnp.where(even, held[1], held[0])], axis=1
    )
    weights = [key_weight, value_weight]
    near = exchange(jnp.broadcast_to(chunk[None], (count,) + chunk.shape))
    far = swap_core(near)
    parts = product_near(near, weights, block)
    same = (core == replica).astype(jnp.int32).reshape(1)
    key_out, value_out, key_own, value_own = product_far(same, far, weights, parts)
    key_in = swap_replica(key_out)
    value_in = swap_replica_lent(lend(value_out))

    query, grad = queries[0, 0], cotangent[0, 0]
    keys, values, low, dscores, grads = attend(
        key_own, key_in, value_own, value_in, query, grad
    )
    grads_in = swap_replica(grads)
    keep = decoder.astype(jnp.int32).reshape(1)
    context, query_grad = attend_out(keep, low, values, dscores, keys)


    weights_far = swap_core(other_rows(core_index, key_weight, value_weight, block, grads))

    def reduce(term):
        return jnp.sum(exchange(term).astype(F32), axis=0)

    grads_over = swap_core(grads)
    own_total = reduce(
        back_product_near(
            core_index, grads, grads_over, *weights, weights_far, block, count
        )
    )
    other_term = back_product(
        core_index, grads_in, swap_core(grads_in), *weights, weights_far, block, count
    )
    other_term, own_total = lax.optimization_barrier((other_term, own_total))
    other_total = reduce(other_term)
    total = jnp.stack([own_total, other_total]).reshape(replicas, rows, 2, block)

    def owned(owner):
        one = lax.dynamic_index_in_dim(total, (owner // 2) ^ replica, 0, keepdims=False)
        return lax.dynamic_index_in_dim(one, owner % 2, 1, keepdims=False)

    summed = None
    for n in range(chips):
        part = send(owned(chip ^ n).astype(BF16), functools.partial(cross_back, n=n))
        part = part.astype(F32)
        summed = part if summed is None else summed + part
    summed = summed.astype(BF16)
    pairs = [
        (place(first + k, d, t), place(first + k - 1, d, t)) for k, d, t in everyone if k % 2
    ]
    summed = jnp.concatenate([summed, lax.ppermute(summed, AXES, pairs)], axis=0)
    out = []
    for k in range(0, count, 2):
        pairs = [
            (place(first + k, d, t), place(root, d, t))
            for d in range(replicas)
            for t in range(lanes)
        ]
        out.append(lax.ppermute(summed, AXES, pairs))
    encoder_grad = jnp.concatenate(out, axis=0)
    encoder_grad = jnp.where(section == root, encoder_grad, jnp.zeros_like(encoder_grad))
    return context[None, None], query_grad[None, None], encoder_grad[None, None]


def solution(mesh):
    wide = P("pipe", "dp", None, "tensor")
    tall = P("pipe", "dp", "tensor")
    return jax.shard_map(
        body,
        mesh=mesh,
        in_specs=(wide, tall, tall, wide, wide),
        out_specs=(wide, wide, wide),
        check_vma=False,
    )
```

```python
import functools

import jax
import jax.numpy as jnp
from jax import lax
from jax.experimental import pallas as pl
from jax.experimental.pallas import tpu as pltpu
from jax.sharding import PartitionSpec as P

HD = 128
AXES = ("pipe", "dp", "tensor")
F32 = jnp.float32
BF16 = jnp.bfloat16
SCALE = HD ** (-0.5)
VMEM = 20 * 1024 * 1024
VMEM_BACK = 48 * 1024 * 1024
NT = (((1,), (1,)), ((), ()))
TN = (((0,), (0,)), ((), ()))


def params():
    return pltpu.CompilerParams(vmem_limit_bytes=VMEM)


def like(shape, dtype):
    return jax.ShapeDtypeStruct(shape, dtype)


def dot(a, b, dims=(((1,), (0,)), ((), ()))):
    return lax.dot_general(a, b, dims, preferred_element_type=F32)


def cost():
    return pl.CostEstimate(flops=1, bytes_accessed=1, transcendentals=0)


def whole(count):
    return [pl.BlockSpec(memory_space=pltpu.VMEM)] * count


def scalar():
    return [pl.BlockSpec(memory_space=pltpu.SMEM)]


def rows_of(weight, index, size):
    return weight[pl.ds(pl.multiple_of(index * size, size), size), :]


def product_near(near, weight):
    count, rows, width = near.shape
    tokens = count * rows
    cols = weight.shape[1]

    def kernel(x_ref, w, out):
        out[...] = dot(x_ref[...].reshape(tokens, width), w[...])

    return pl.pallas_call(
        kernel,
        in_specs=whole(2),
        out_specs=whole(1)[0],
        out_shape=like((tokens, cols), F32),
        cost_estimate=cost(),
        compiler_params=params(),
    )(near, weight)


def product_far(same, far, weights, parts, block):
    count, rows, width = far.shape
    tokens = count * rows
    cols = weights[0].shape[1]
    steps = width // block

    def kernel(same_ref, far_ref, wk, wv, pk, pv, key_out, value_out, key_own, value_own, x, sems):
        same_here = same_ref[0] > 0
        loads = []
        for i in range(steps):
            at = pl.ds(i * block, block)
            loads.append(
                pltpu.make_async_copy(far_ref.at[:, :, at], x.at[:, :, at], sems.at[i])
            )
        for load in loads:
            load.start()
        totals = [None, None]
        for i in range(steps):
            loads[i].wait()
            at = slice(i * block, (i + 1) * block)
            here = x[:, :, at].reshape(tokens, block)
            for n, w in enumerate((wk, wv)):
                term = dot(here, w[at, :])
                totals[n] = term if i == 0 else totals[n] + term
        for total, p, out, own in (
            (totals[0], pk, key_out, key_own),
            (totals[1], pv, value_out, value_own),
        ):
            part = p[...]
            out[...] = jnp.where(same_here, total, part).astype(out.dtype)
            own[...] = jnp.where(same_here, part, total)

    return pl.pallas_call(
        kernel,
        in_specs=scalar() + [pl.BlockSpec(memory_space=pl.ANY)] + whole(4),
        out_specs=whole(4),
        out_shape=[like((tokens, cols), t) for t in (F32, BF16, F32, F32)],
        scratch_shapes=[
            pltpu.VMEM((count, rows, width), BF16),
            pltpu.SemaphoreType.DMA((steps,)),
        ],
        cost_estimate=cost(),
        compiler_params=params(),
    )(same, far, *weights, *parts)


def settle(array, after):
    def kernel(source, after_ref, out):
        out[...] = source[...]

    return pl.pallas_call(
        kernel,
        in_specs=whole(1) + [pl.BlockSpec(memory_space=pl.ANY)],
        out_specs=whole(1)[0],
        out_shape=like(array.shape, array.dtype),
        cost_estimate=cost(),
        compiler_params=params(),
    )(array, after)


def other_rows(core, key_weight, value_weight, grads, block):
    height, cols = key_weight.shape
    tokens = grads.shape[0]

    def kernel(core_ref, wk, wv, g, out):
        c = 1 - core_ref[0]
        for n, w in enumerate((wk, wv)):
            for j in range(2):
                at = (2 * n + j) * block
                out[at : at + block, :] = rows_of(w, 2 * j + c, block)
            at = 2 * height // 2 + n * tokens
            out[at : at + tokens, :] = g[:, n * cols : (n + 1) * cols]

    return pl.pallas_call(
        kernel,
        in_specs=scalar() + whole(3),
        out_specs=whole(1)[0],
        out_shape=like((height + 2 * tokens, cols), BF16),
        cost_estimate=cost(),
        compiler_params=params(),
    )(core, key_weight, value_weight, grads)


def attend(key_own, key_in, value_own, value_in, query, grad):
    tokens, local = key_own.shape
    dec = query.shape[0]
    heads = local // HD

    def kernel(ka, kb, va, vb, q, g, keys, values, low, dscores, grads):
        for h in range(heads):
            at = slice(h * HD, (h + 1) * HD)
            k = (ka[:, at] + kb[:, at]).astype(BF16)
            v = (va[:, at] + vb[:, at].astype(F32)).astype(BF16)
            keys[:, at] = k
            values[:, at] = v
            scores = dot(q[:, at], k, NT) * SCALE
            top = jnp.max(scores, axis=-1, keepdims=True)
            e = jnp.exp(scores - top)
            p = e / jnp.sum(e, axis=-1, keepdims=True)
            rounded = p.astype(BF16)
            low[h] = rounded
            dprobs = dot(g[:, at], v, NT)
            delta = jnp.sum(p * dprobs, axis=-1, keepdims=True)
            ds = (p * (dprobs - delta) * SCALE).astype(BF16)
            dscores[h] = ds
            grads[:, at] = dot(ds, q[:, at], TN).astype(BF16)
            start = local + h * HD
            grads[:, start : start + HD] = dot(rounded, g[:, at], TN).astype(BF16)

    return pl.pallas_call(
        kernel,
        in_specs=whole(6),
        out_specs=whole(5),
        out_shape=[
            like((tokens, local), BF16),
            like((tokens, local), BF16),
            like((heads, dec, tokens), BF16),
            like((heads, dec, tokens), BF16),
            like((tokens, 2 * local), BF16),
        ],
        cost_estimate=cost(),
        compiler_params=params(),
    )(key_own, key_in, value_own, value_in, query, grad)


def attend_out(keep, low, values, dscores, keys):
    tokens, local = values.shape
    heads, dec = low.shape[:2]

    def kernel(keep_ref, p, v, ds, k, context, query_grad):
        on = keep_ref[0] > 0
        for h in range(heads):
            at = slice(h * HD, (h + 1) * HD)
            context[:, at] = jnp.where(on, dot(p[h], v[:, at]), 0.0).astype(BF16)
            query_grad[:, at] = jnp.where(on, dot(ds[h], k[:, at]), 0.0).astype(BF16)

    return pl.pallas_call(
        kernel,
        in_specs=scalar() + whole(4),
        out_specs=whole(2),
        out_shape=[like((dec, local), BF16)] * 2,
        cost_estimate=cost(),
        compiler_params=params(),
    )(keep, low, values, dscores, keys)


def back_product_near(core, mine, key_weight, value_weight, packet, block, count):
    tokens = mine.shape[0]
    cols = key_weight.shape[1]
    width = 2 * block
    step = block // 2
    rows = tokens // count

    def kernel(core_ref, g, wk, wv, far, out, low, sems):
        c = core_ref[0]
        copies = []
        for i in range(width // step):
            at = (i // 2 * 2 + c) * 2 + i % 2
            total = dot(g[:, :cols], rows_of(wk, at, step), NT)
            total += dot(g[:, cols:], rows_of(wv, at, step), NT)
            for n in range(2):
                weight = far[n * width + i * step : n * width + (i + 1) * step, :]
                at = 2 * width + n * tokens
                total += dot(far[at : at + tokens, :], weight, NT)
            low[i] = total.reshape(count, rows, step).astype(BF16)
            copy = pltpu.make_async_copy(
                low.at[i], out.at[:, :, pl.ds(i * step, step)], sems.at[i]
            )
            copy.start()
            copies.append(copy)
        for copy in copies:
            copy.wait()

    return pl.pallas_call(
        kernel,
        in_specs=scalar() + whole(4),
        out_specs=pl.BlockSpec(memory_space=pltpu.HBM),
        out_shape=like((count, rows, width), BF16),
        scratch_shapes=[
            pltpu.VMEM((width // step, count, rows, step), BF16),
            pltpu.SemaphoreType.DMA((width // step,)),
        ],
        cost_estimate=cost(),
        compiler_params=params(),
    )(core, mine, key_weight, value_weight, packet)


def back_product(core, mine, others, key_weight, value_weight, packet, block, count):
    tokens = mine.shape[0]
    cols = key_weight.shape[1]
    width = 2 * block
    step = block // 2
    steps = width // step
    rows = tokens // count

    def kernel(core_ref, g, h, wk, wv, far, out, held, low, in_sems, out_sems):
        c = core_ref[0]
        loads = []
        for i in range(steps):
            at = pl.ds(pl.multiple_of(((i // 2 * 2 + c) * 2 + i % 2) * step, step), step)
            sources = [wk.at[at], wv.at[at]]
            sources += [far.at[pl.ds(n * width + i * step, step)] for n in range(2)]
            loads.append(
                [
                    pltpu.make_async_copy(source, held.at[i, n], in_sems.at[i, n])
                    for n, source in enumerate(sources)
                ]
            )
        for group in loads:
            for load in group:
                load.start()
        stores = []
        for i in range(steps):
            total = None
            for n, a in enumerate((g, g, h, h)):
                loads[i][n].wait()
                term = dot(a[:, n % 2 * cols : (n % 2 + 1) * cols], held[i, n], NT)
                total = term if total is None else total + term
            low[i] = total.reshape(count, rows, step).astype(BF16)
            store = pltpu.make_async_copy(
                low.at[i], out.at[:, :, pl.ds(i * step, step)], out_sems.at[i]
            )
            store.start()
            stores.append(store)
        for store in stores:
            store.wait()

    return pl.pallas_call(
        kernel,
        in_specs=scalar() + whole(2) + [pl.BlockSpec(memory_space=pl.ANY)] * 3,
        out_specs=pl.BlockSpec(memory_space=pl.ANY),
        out_shape=like((count, rows, width), BF16),
        scratch_shapes=[
            pltpu.VMEM((steps, 4, step, cols), BF16),
            pltpu.VMEM((steps, count, rows, step), BF16),
            pltpu.SemaphoreType.DMA((steps, 4)),
            pltpu.SemaphoreType.DMA((steps,)),
        ],
        cost_estimate=cost(),
        compiler_params=pltpu.CompilerParams(vmem_limit_bytes=VMEM_BACK),
    )(core, mine, others, key_weight, value_weight, packet)


def body(section_states, key_weight, value_weight, queries, cotangent):
    sections = lax.axis_size("pipe")
    replicas = lax.axis_size("dp")
    lanes = lax.axis_size("tensor")
    first = sections // 2
    count = sections - first
    root = first - 1
    section = lax.axis_index("pipe")
    replica = lax.axis_index("dp")
    lane = lax.axis_index("tensor")
    core = lane % 2
    chip = lane // 2
    chips = lanes // 2
    decoder = section >= first
    half = lanes // 2

    def place(s, d, t):
        return (s * replicas + d) * lanes + t

    everyone = [(k, d, t) for k in range(count) for d in range(replicas) for t in range(lanes)]

    def send(array, move):
        pairs = []
        for k, d, t in everyone:
            a, b, c = move(k, d, t)
            pairs.append((place(first + k, d, t), place(first + a, b, c)))
        return lax.ppermute(array, AXES, pairs)

    def swap_core(array):
        return send(array, lambda k, d, t: (k, d, t ^ 1))

    def swap_replica(array):
        return send(array, lambda k, d, t: (k, 1 - d, t))

    def beside(k, d, t):
        return place((k + count // 2) % count, d, t)

    def lend(array):
        pairs = [(place(first + k, d, t), beside(k, d, t)) for k, d, t in everyone]
        return lax.ppermute(array, AXES, pairs)

    def swap_replica_lent(array):
        pairs = [(beside(k, d, t), place(first + k, 1 - d, t)) for k, d, t in everyone]
        return lax.ppermute(array, AXES, pairs)

    groups = [list(range(first)), list(range(first, sections))]

    def exchange(array):
        return lax.all_to_all(array, "pipe", 0, 0, axis_index_groups=groups)

    def cross(k, d, t, n):
        over = 2 * (t % 2) + (n ^ (t % half) // 2)
        return (k, t // half, 2 * over + d)

    def cross_back(k, d, t, n):
        owner = (t // 2) ^ n
        return (k, owner // 2, half * d + 2 * (owner % 2) + t % 2)

    def in_order(mine, others):
        return jnp.where(core == 0, mine, others), jnp.where(core == 0, others, mine)

    piece = section_states[0, 0]
    key_weight, value_weight = key_weight[0], value_weight[0]
    tokens, block = piece.shape
    rows = tokens // count
    local = key_weight.shape[1]
    core_index = core.astype(jnp.int32).reshape(1)

    got = None
    for k in range(count):
        pairs = [
            (place(root, d, t), place(first + k, d, t))
            for d in range(replicas)
            for t in range(lanes)
        ]
        part = lax.ppermute(piece[k * rows : (k + 1) * rows], AXES, pairs)
        got = part if got is None else got + part
    both = jnp.concatenate(in_order(got, swap_core(got)), axis=1)
    held = [send(both, functools.partial(cross, n=n)) for n in range(2)]
    even = chip % 2 == 0
    chunk = jnp.concatenate(
        [jnp.where(even, held[0], held[1]), jnp.where(even, held[1], held[0])], axis=1
    )
    weights = [key_weight, value_weight]
    near = exchange(jnp.broadcast_to(chunk[None], (count,) + chunk.shape))
    far = swap_core(near)
    parts = [product_near(near, weight) for weight in weights]
    same = (core == replica).astype(jnp.int32).reshape(1)
    key_out, value_out, key_own, value_own = product_far(same, far, weights, parts, block)
    key_in = swap_replica(key_out)
    lent = lend(value_out)
    value_in = swap_replica_lent(lent)
    key_own = settle(key_own, lent)

    query, grad = queries[0, 0], cotangent[0, 0]
    keys, values, low, dscores, grads = attend(
        key_own, key_in, value_own, value_in, query, grad
    )
    grads_in = swap_replica(grads)
    keep = decoder.astype(jnp.int32).reshape(1)
    context, query_grad = attend_out(keep, low, values, dscores, keys)


    packet = swap_core(other_rows(core_index, *weights, grads, block))

    own_terms = exchange(
        back_product_near(core_index, grads, *weights, packet, block, count)
    )
    other_term = back_product(
        core_index, grads_in, swap_core(grads_in), *weights, packet, block, count
    )
    other_term, own_terms = lax.optimization_barrier((other_term, own_terms))
    own_total, other_total = (
        jnp.sum(terms.astype(F32), axis=0) for terms in (own_terms, exchange(other_term))
    )
    total = jnp.stack([own_total, other_total]).reshape(replicas, rows, 2, block)

    def owned(owner):
        one = lax.dynamic_index_in_dim(total, (owner // 2) ^ replica, 0, keepdims=False)
        return lax.dynamic_index_in_dim(one, owner % 2, 1, keepdims=False)

    summed = None
    for n in range(chips):
        part = send(owned(chip ^ n).astype(BF16), functools.partial(cross_back, n=n))
        part = part.astype(F32)
        summed = part if summed is None else summed + part
    summed = summed.astype(BF16)
    pairs = [
        (place(first + k, d, t), place(first + k - 1, d, t)) for k, d, t in everyone if k % 2
    ]
    summed = jnp.concatenate([summed, lax.ppermute(summed, AXES, pairs)], axis=0)
    out = []
    for k in range(0, count, 2):
        pairs = [
            (place(first + k, d, t), place(root, d, t))
            for d in range(replicas)
            for t in range(lanes)
        ]
        out.append(lax.ppermute(summed, AXES, pairs))
    encoder_grad = jnp.concatenate(out, axis=0)
    encoder_grad = jnp.where(section == root, encoder_grad, jnp.zeros_like(encoder_grad))
    return context[None, None], query_grad[None, None], encoder_grad[None, None]


def solution(mesh):
    wide = P("pipe", "dp", None, "tensor")
    tall = P("pipe", "dp", "tensor")
    return jax.shard_map(
        body,
        mesh=mesh,
        in_specs=(wide, tall, tall, wide, wide),
        out_specs=(wide, wide, wide),
        check_vma=False,
    )
```

```python
import functools

import jax
import jax.numpy as jnp
from jax import lax
from jax.experimental import pallas as pl
from jax.experimental.pallas import tpu as pltpu
from jax.sharding import PartitionSpec as P

HD = 128
AXES = ("pipe", "dp", "tensor")
F32 = jnp.float32
BF16 = jnp.bfloat16
SCALE = HD ** (-0.5)
VMEM = 20 * 1024 * 1024
VMEM_BACK = 48 * 1024 * 1024
NT = (((1,), (1,)), ((), ()))
TN = (((0,), (0,)), ((), ()))


def params():
    return pltpu.CompilerParams(vmem_limit_bytes=VMEM)


def like(shape, dtype):
    return jax.ShapeDtypeStruct(shape, dtype)


def dot(a, b, dims=(((1,), (0,)), ((), ()))):
    return lax.dot_general(a, b, dims, preferred_element_type=F32)


def cost():
    return pl.CostEstimate(flops=1, bytes_accessed=1, transcendentals=0)


def whole(count):
    return [pl.BlockSpec(memory_space=pltpu.VMEM)] * count


def scalar():
    return [pl.BlockSpec(memory_space=pltpu.SMEM)]


def rows_of(weight, index, size):
    return weight[pl.ds(pl.multiple_of(index * size, size), size), :]


def product_near(near, weight):
    count, rows, width = near.shape
    tokens = count * rows
    cols = weight.shape[1]

    def kernel(x_ref, w, out):
        out[...] = dot(x_ref[...].reshape(tokens, width), w[...])

    return pl.pallas_call(
        kernel,
        in_specs=whole(2),
        out_specs=whole(1)[0],
        out_shape=like((tokens, cols), F32),
        cost_estimate=cost(),
        compiler_params=params(),
    )(near, weight)


def product_far(same, far, weights, parts, block):
    count, rows, width = far.shape
    tokens = count * rows
    cols = weights[0].shape[1]
    steps = width // block

    def kernel(same_ref, far_ref, wk, wv, pk, pv, key_out, value_out, key_own, value_own, x, sems):
        same_here = same_ref[0] > 0
        loads = []
        for i in range(steps):
            at = pl.ds(i * block, block)
            loads.append(
                pltpu.make_async_copy(far_ref.at[:, :, at], x.at[:, :, at], sems.at[i])
            )
        for load in loads:
            load.start()
        totals = [None, None]
        for i in range(steps):
            loads[i].wait()
            at = slice(i * block, (i + 1) * block)
            here = x[:, :, at].reshape(tokens, block)
            for n, w in enumerate((wk, wv)):
                term = dot(here, w[at, :])
                totals[n] = term if i == 0 else totals[n] + term
        for total, p, out, own in (
            (totals[0], pk, key_out, key_own),
            (totals[1], pv, value_out, value_own),
        ):
            part = p[...]
            out[...] = jnp.where(same_here, total, part).astype(out.dtype)
            own[...] = jnp.where(same_here, part, total)

    return pl.pallas_call(
        kernel,
        in_specs=scalar() + [pl.BlockSpec(memory_space=pl.ANY)] + whole(4),
        out_specs=whole(4),
        out_shape=[like((tokens, cols), t) for t in (F32, BF16, F32, F32)],
        scratch_shapes=[
            pltpu.VMEM((count, rows, width), BF16),
            pltpu.SemaphoreType.DMA((steps,)),
        ],
        cost_estimate=cost(),
        compiler_params=params(),
    )(same, far, *weights, *parts)


def settle(array, after):
    def kernel(source, after_ref, out):
        out[...] = source[...]

    return pl.pallas_call(
        kernel,
        in_specs=whole(1) + [pl.BlockSpec(memory_space=pl.ANY)],
        out_specs=whole(1)[0],
        out_shape=like(array.shape, array.dtype),
        cost_estimate=cost(),
        compiler_params=params(),
    )(array, after)


def other_rows(core, key_weight, value_weight, grads, block):
    height, cols = key_weight.shape
    tokens = grads.shape[0]

    def kernel(core_ref, wk, wv, g, out):
        c = 1 - core_ref[0]
        for n, w in enumerate((wk, wv)):
            for j in range(2):
                at = (2 * n + j) * block
                out[at : at + block, :] = rows_of(w, 2 * j + c, block)
            at = 2 * height // 2 + n * tokens
            out[at : at + tokens, :] = g[:, n * cols : (n + 1) * cols]

    return pl.pallas_call(
        kernel,
        in_specs=scalar() + whole(3),
        out_specs=whole(1)[0],
        out_shape=like((height + 2 * tokens, cols), BF16),
        cost_estimate=cost(),
        compiler_params=params(),
    )(core, key_weight, value_weight, grads)


def attend(key_own, key_in, value_own, value_in, query, grad):
    tokens, local = key_own.shape
    dec = query.shape[0]
    heads = local // HD

    def kernel(ka, kb, va, vb, q, g, keys, values, low, dscores, grads):
        for h in range(heads):
            at = slice(h * HD, (h + 1) * HD)
            k = (ka[:, at] + kb[:, at]).astype(BF16)
            v = (va[:, at] + vb[:, at].astype(F32)).astype(BF16)
            keys[:, at] = k
            values[:, at] = v
            scores = dot(q[:, at], k, NT) * SCALE
            top = jnp.max(scores, axis=-1, keepdims=True)
            e = jnp.exp(scores - top)
            p = e / jnp.sum(e, axis=-1, keepdims=True)
            rounded = p.astype(BF16)
            low[h] = rounded
            dprobs = dot(g[:, at], v, NT)
            delta = jnp.sum(p * dprobs, axis=-1, keepdims=True)
            ds = (p * (dprobs - delta) * SCALE).astype(BF16)
            dscores[h] = ds
            grads[:, at] = dot(ds, q[:, at], TN).astype(BF16)
            start = local + h * HD
            grads[:, start : start + HD] = dot(rounded, g[:, at], TN).astype(BF16)

    return pl.pallas_call(
        kernel,
        in_specs=whole(6),
        out_specs=whole(5),
        out_shape=[
            like((tokens, local), BF16),
            like((tokens, local), BF16),
            like((heads, dec, tokens), BF16),
            like((heads, dec, tokens), BF16),
            like((tokens, 2 * local), BF16),
        ],
        cost_estimate=cost(),
        compiler_params=params(),
    )(key_own, key_in, value_own, value_in, query, grad)


def attend_out(keep, low, values, dscores, keys):
    tokens, local = values.shape
    heads, dec = low.shape[:2]

    def kernel(keep_ref, p, v, ds, k, context, query_grad):
        on = keep_ref[0] > 0
        for h in range(heads):
            at = slice(h * HD, (h + 1) * HD)
            context[:, at] = jnp.where(on, dot(p[h], v[:, at]), 0.0).astype(BF16)
            query_grad[:, at] = jnp.where(on, dot(ds[h], k[:, at]), 0.0).astype(BF16)

    return pl.pallas_call(
        kernel,
        in_specs=scalar() + whole(4),
        out_specs=whole(2),
        out_shape=[like((dec, local), BF16)] * 2,
        cost_estimate=cost(),
        compiler_params=params(),
    )(keep, low, values, dscores, keys)


def back_product_near(core, mine, key_weight, value_weight, packet, block, count):
    tokens = mine.shape[0]
    cols = key_weight.shape[1]
    width = 2 * block
    step = block // 2
    rows = tokens // count

    def kernel(core_ref, g, wk, wv, far, out, low, sems):
        c = core_ref[0]
        copies = []
        for i in range(width // step):
            at = (i // 2 * 2 + c) * 2 + i % 2
            total = dot(g[:, :cols], rows_of(wk, at, step), NT)
            total += dot(g[:, cols:], rows_of(wv, at, step), NT)
            for n in range(2):
                weight = far[n * width + i * step : n * width + (i + 1) * step, :]
                at = 2 * width + n * tokens
                total += dot(far[at : at + tokens, :], weight, NT)
            low[i] = total.reshape(count, rows, step).astype(BF16)
            copy = pltpu.make_async_copy(
                low.at[i], out.at[:, :, pl.ds(i * step, step)], sems.at[i]
            )
            copy.start()
            copies.append(copy)
        for copy in copies:
            copy.wait()

    return pl.pallas_call(
        kernel,
        in_specs=scalar() + whole(4),
        out_specs=pl.BlockSpec(memory_space=pltpu.HBM),
        out_shape=like((count, rows, width), BF16),
        scratch_shapes=[
            pltpu.VMEM((width // step, count, rows, step), BF16),
            pltpu.SemaphoreType.DMA((width // step,)),
        ],
        cost_estimate=cost(),
        compiler_params=params(),
    )(core, mine, key_weight, value_weight, packet)


def back_part(core, mine, key_weight, value_weight, block):
    tokens = mine.shape[0]
    cols = key_weight.shape[1]
    step = block // 2
    steps = 2 * block // step

    def kernel(core_ref, g, wk, wv, out, held, sems):
        c = core_ref[0]
        loads = []
        for i in range(steps):
            at = pl.ds(pl.multiple_of(((i // 2 * 2 + c) * 2 + i % 2) * step, step), step)
            loads.append(
                [
                    pltpu.make_async_copy(w.at[at], held.at[i, n], sems.at[i, n])
                    for n, w in enumerate((wk, wv))
                ]
            )
        for group in loads:
            for load in group:
                load.start()
        for i in range(steps):
            total = None
            for n in range(2):
                loads[i][n].wait()
                term = dot(g[:, n * cols : (n + 1) * cols], held[i, n], NT)
                total = term if total is None else total + term
            out[i] = total

    return pl.pallas_call(
        kernel,
        in_specs=scalar() + whole(1) + [pl.BlockSpec(memory_space=pl.ANY)] * 2,
        out_specs=whole(1)[0],
        out_shape=like((steps, tokens, step), F32),
        scratch_shapes=[
            pltpu.VMEM((steps, 2, step, cols), BF16),
            pltpu.SemaphoreType.DMA((steps, 2)),
        ],
        cost_estimate=cost(),
        compiler_params=pltpu.CompilerParams(vmem_limit_bytes=VMEM_BACK),
    )(core, mine, key_weight, value_weight)


def back_rest(part, others, packet, block, count):
    steps, tokens, step = part.shape
    cols = packet.shape[1]
    width = 2 * block
    rows = tokens // count

    def kernel(p, h, far, out, held, low, in_sems, out_sems):
        loads = [
            [
                pltpu.make_async_copy(
                    far.at[pl.ds(n * width + i * step, step)], held.at[i, n], in_sems.at[i, n]
                )
                for n in range(2)
            ]
            for i in range(steps)
        ]
        for group in loads:
            for load in group:
                load.start()
        stores = []
        for i in range(steps):
            total = p[i]
            for n in range(2):
                loads[i][n].wait()
                total = total + dot(h[:, n * cols : (n + 1) * cols], held[i, n], NT)
            low[i] = total.reshape(count, rows, step).astype(BF16)
            store = pltpu.make_async_copy(
                low.at[i], out.at[:, :, pl.ds(i * step, step)], out_sems.at[i]
            )
            store.start()
            stores.append(store)
        for store in stores:
            store.wait()

    return pl.pallas_call(
        kernel,
        in_specs=whole(2) + [pl.BlockSpec(memory_space=pl.ANY)],
        out_specs=pl.BlockSpec(memory_space=pl.ANY),
        out_shape=like((count, rows, width), BF16),
        scratch_shapes=[
            pltpu.VMEM((steps, 2, step, cols), BF16),
            pltpu.VMEM((steps, count, rows, step), BF16),
            pltpu.SemaphoreType.DMA((steps, 2)),
            pltpu.SemaphoreType.DMA((steps,)),
        ],
        cost_estimate=cost(),
        compiler_params=pltpu.CompilerParams(vmem_limit_bytes=VMEM_BACK),
    )(part, others, packet)


def body(section_states, key_weight, value_weight, queries, cotangent):
    sections = lax.axis_size("pipe")
    replicas = lax.axis_size("dp")
    lanes = lax.axis_size("tensor")
    first = sections // 2
    count = sections - first
    root = first - 1
    section = lax.axis_index("pipe")
    replica = lax.axis_index("dp")
    lane = lax.axis_index("tensor")
    core = lane % 2
    chip = lane // 2
    chips = lanes // 2
    decoder = section >= first
    half = lanes // 2

    def place(s, d, t):
        return (s * replicas + d) * lanes + t

    everyone = [(k, d, t) for k in range(count) for d in range(replicas) for t in range(lanes)]

    def send(array, move):
        pairs = []
        for k, d, t in everyone:
            a, b, c = move(k, d, t)
            pairs.append((place(first + k, d, t), place(first + a, b, c)))
        return lax.ppermute(array, AXES, pairs)

    def swap_core(array):
        return send(array, lambda k, d, t: (k, d, t ^ 1))

    def swap_replica(array):
        return send(array, lambda k, d, t: (k, 1 - d, t))

    def beside(k, d, t):
        return place((k + count // 2) % count, d, t)

    def lend(array):
        pairs = [(place(first + k, d, t), beside(k, d, t)) for k, d, t in everyone]
        return lax.ppermute(array, AXES, pairs)

    def swap_replica_lent(array):
        pairs = [(beside(k, d, t), place(first + k, 1 - d, t)) for k, d, t in everyone]
        return lax.ppermute(array, AXES, pairs)

    groups = [list(range(first)), list(range(first, sections))]

    def exchange(array):
        return lax.all_to_all(array, "pipe", 0, 0, axis_index_groups=groups)

    def cross(k, d, t, n):
        over = 2 * (t % 2) + (n ^ (t % half) // 2)
        return (k, t // half, 2 * over + d)

    def cross_back(k, d, t, n):
        owner = (t // 2) ^ n
        return (k, owner // 2, half * d + 2 * (owner % 2) + t % 2)

    def in_order(mine, others):
        return jnp.where(core == 0, mine, others), jnp.where(core == 0, others, mine)

    piece = section_states[0, 0]
    key_weight, value_weight = key_weight[0], value_weight[0]
    tokens, block = piece.shape
    rows = tokens // count
    local = key_weight.shape[1]
    core_index = core.astype(jnp.int32).reshape(1)

    got = None
    for k in range(count):
        pairs = [
            (place(root, d, t), place(first + k, d, t))
            for d in range(replicas)
            for t in range(lanes)
        ]
        part = lax.ppermute(piece[k * rows : (k + 1) * rows], AXES, pairs)
        got = part if got is None else got + part
    both = jnp.concatenate(in_order(got, swap_core(got)), axis=1)
    held = [send(both, functools.partial(cross, n=n)) for n in range(2)]
    even = chip % 2 == 0
    chunk = jnp.concatenate(
        [jnp.where(even, held[0], held[1]), jnp.where(even, held[1], held[0])], axis=1
    )
    weights = [key_weight, value_weight]
    near = exchange(jnp.broadcast_to(chunk[None], (count,) + chunk.shape))
    far = swap_core(near)
    parts = [product_near(near, weight) for weight in weights]
    same = (core == replica).astype(jnp.int32).reshape(1)
    key_out, value_out, key_own, value_own = product_far(same, far, weights, parts, block)
    key_in = swap_replica(key_out)
    lent = lend(value_out)
    value_in = swap_replica_lent(lent)
    key_own = settle(key_own, lent)

    query, grad = queries[0, 0], cotangent[0, 0]
    keys, values, low, dscores, grads = attend(
        key_own, key_in, value_own, value_in, query, grad
    )
    grads_in = swap_replica(grads)
    keep = decoder.astype(jnp.int32).reshape(1)
    context, query_grad = attend_out(keep, low, values, dscores, keys)


    packet = swap_core(other_rows(core_index, *weights, grads, block))

    own_terms = exchange(
        back_product_near(core_index, grads, *weights, packet, block, count)
    )
    other_part = back_part(core_index, grads_in, *weights, block)
    other_term = back_rest(other_part, swap_core(grads_in), packet, block, count)
    other_term, own_terms = lax.optimization_barrier((other_term, own_terms))
    own_total, other_total = (
        jnp.sum(terms.astype(F32), axis=0) for terms in (own_terms, exchange(other_term))
    )
    total = jnp.stack([own_total, other_total]).reshape(replicas, rows, 2, block)

    def owned(owner):
        one = lax.dynamic_index_in_dim(total, (owner // 2) ^ replica, 0, keepdims=False)
        return lax.dynamic_index_in_dim(one, owner % 2, 1, keepdims=False)

    summed = None
    for n in range(chips):
        part = send(owned(chip ^ n).astype(BF16), functools.partial(cross_back, n=n))
        part = part.astype(F32)
        summed = part if summed is None else summed + part
    summed = summed.astype(BF16)
    pairs = [
        (place(first + k, d, t), place(first + k - count // 2, d, t)) for k, d, t in everyone if k >= count // 2
    ]
    summed = jnp.concatenate([summed, lax.ppermute(summed, AXES, pairs)], axis=0)
    out = []
    for k in range(count // 2):
        pairs = [
            (place(first + k, d, t), place(root, d, t))
            for d in range(replicas)
            for t in range(lanes)
        ]
        out.append(lax.ppermute(summed, AXES, pairs))
    encoder_grad = jnp.concatenate([o[:rows] for o in out] + [o[rows:] for o in out], axis=0)
    encoder_grad = jnp.where(section == root, encoder_grad, jnp.zeros_like(encoder_grad))
    return context[None, None], query_grad[None, None], encoder_grad[None, None]


def solution(mesh):
    wide = P("pipe", "dp", None, "tensor")
    tall = P("pipe", "dp", "tensor")
    return jax.shard_map(
        body,
        mesh=mesh,
        in_specs=(wide, tall, tall, wide, wide),
        out_specs=(wide, wide, wide),
        check_vma=False,
    )
```

```python
import functools

import jax
import jax.numpy as jnp
from jax import lax
from jax.experimental import pallas as pl
from jax.experimental.pallas import tpu as pltpu
from jax.sharding import PartitionSpec as P

HD = 128
AXES = ("pipe", "dp", "tensor")
F32 = jnp.float32
BF16 = jnp.bfloat16
SCALE = HD ** (-0.5)
VMEM = 20 * 1024 * 1024
VMEM_BACK = 48 * 1024 * 1024
NT = (((1,), (1,)), ((), ()))
TN = (((0,), (0,)), ((), ()))


def params():
    return pltpu.CompilerParams(vmem_limit_bytes=VMEM)


def like(shape, dtype):
    return jax.ShapeDtypeStruct(shape, dtype)


def dot(a, b, dims=(((1,), (0,)), ((), ()))):
    return lax.dot_general(a, b, dims, preferred_element_type=F32)


def cost():
    return pl.CostEstimate(flops=1, bytes_accessed=1, transcendentals=0)


def whole(count):
    return [pl.BlockSpec(memory_space=pltpu.VMEM)] * count


def scalar():
    return [pl.BlockSpec(memory_space=pltpu.SMEM)]


def rows_of(weight, index, size):
    return weight[pl.ds(pl.multiple_of(index * size, size), size), :]


def product_near(near, weight):
    count, rows, width = near.shape
    tokens = count * rows
    cols = weight.shape[1]

    def kernel(x_ref, w, out):
        out[...] = dot(x_ref[...].reshape(tokens, width), w[...])

    return pl.pallas_call(
        kernel,
        in_specs=whole(2),
        out_specs=whole(1)[0],
        out_shape=like((tokens, cols), F32),
        cost_estimate=cost(),
        compiler_params=params(),
    )(near, weight)


def product_far(same, far, weights, parts, block):
    count, rows, width = far.shape
    tokens = count * rows
    cols = weights[0].shape[1]
    steps = width // block

    def kernel(same_ref, far_ref, wk, wv, pk, pv, key_out, value_out, key_own, value_own, x, sems):
        same_here = same_ref[0] > 0
        loads = []
        for i in range(steps):
            at = pl.ds(i * block, block)
            loads.append(
                pltpu.make_async_copy(far_ref.at[:, :, at], x.at[:, :, at], sems.at[i])
            )
        for load in loads:
            load.start()
        totals = [None, None]
        for i in range(steps):
            loads[i].wait()
            at = slice(i * block, (i + 1) * block)
            here = x[:, :, at].reshape(tokens, block)
            for n, w in enumerate((wk, wv)):
                term = dot(here, w[at, :])
                totals[n] = term if i == 0 else totals[n] + term
        for total, p, out, own in (
            (totals[0], pk, key_out, key_own),
            (totals[1], pv, value_out, value_own),
        ):
            part = p[...]
            out[...] = jnp.where(same_here, total, part).astype(out.dtype)
            own[...] = jnp.where(same_here, part, total)

    return pl.pallas_call(
        kernel,
        in_specs=scalar() + [pl.BlockSpec(memory_space=pl.ANY)] + whole(4),
        out_specs=whole(4),
        out_shape=[like((tokens, cols), t) for t in (F32, BF16, F32, F32)],
        scratch_shapes=[
            pltpu.VMEM((count, rows, width), BF16),
            pltpu.SemaphoreType.DMA((steps,)),
        ],
        cost_estimate=cost(),
        compiler_params=params(),
    )(same, far, *weights, *parts)


def settle(array, after):
    def kernel(source, after_ref, out):
        out[...] = source[...]

    return pl.pallas_call(
        kernel,
        in_specs=whole(1) + [pl.BlockSpec(memory_space=pl.ANY)],
        out_specs=whole(1)[0],
        out_shape=like(array.shape, array.dtype),
        cost_estimate=cost(),
        compiler_params=params(),
    )(array, after)


def other_rows(core, key_weight, value_weight, grads, block):
    height, cols = key_weight.shape
    tokens = grads.shape[0]

    def kernel(core_ref, wk, wv, g, out):
        c = 1 - core_ref[0]
        for n, w in enumerate((wk, wv)):
            for j in range(2):
                at = (2 * n + j) * block
                out[at : at + block, :] = rows_of(w, 2 * j + c, block)
            at = 2 * height // 2 + n * tokens
            out[at : at + tokens, :] = g[:, n * cols : (n + 1) * cols]

    return pl.pallas_call(
        kernel,
        in_specs=scalar() + whole(3),
        out_specs=whole(1)[0],
        out_shape=like((height + 2 * tokens, cols), BF16),
        cost_estimate=cost(),
        compiler_params=params(),
    )(core, key_weight, value_weight, grads)


def attend(key_own, key_in, value_own, value_in, query, grad):
    tokens, local = key_own.shape
    dec = query.shape[0]
    heads = local // HD

    def kernel(ka, kb, va, vb, q, g, keys, values, low, dscores, grads):
        for h in range(heads):
            at = slice(h * HD, (h + 1) * HD)
            k = (ka[:, at] + kb[:, at]).astype(BF16)
            v = (va[:, at] + vb[:, at].astype(F32)).astype(BF16)
            keys[:, at] = k
            values[:, at] = v
            scores = dot(q[:, at], k, NT) * SCALE
            top = jnp.max(scores, axis=-1, keepdims=True)
            e = jnp.exp(scores - top)
            p = e / jnp.sum(e, axis=-1, keepdims=True)
            rounded = p.astype(BF16)
            low[h] = rounded
            dprobs = dot(g[:, at], v, NT)
            delta = jnp.sum(p * dprobs, axis=-1, keepdims=True)
            ds = (p * (dprobs - delta) * SCALE).astype(BF16)
            dscores[h] = ds
            grads[:, at] = dot(ds, q[:, at], TN).astype(BF16)
            start = local + h * HD
            grads[:, start : start + HD] = dot(rounded, g[:, at], TN).astype(BF16)

    return pl.pallas_call(
        kernel,
        in_specs=whole(6),
        out_specs=whole(5),
        out_shape=[
            like((tokens, local), BF16),
            like((tokens, local), BF16),
            like((heads, dec, tokens), BF16),
            like((heads, dec, tokens), BF16),
            like((tokens, 2 * local), BF16),
        ],
        cost_estimate=cost(),
        compiler_params=params(),
    )(key_own, key_in, value_own, value_in, query, grad)


def attend_out(keep, low, values, dscores, keys):
    tokens, local = values.shape
    heads, dec = low.shape[:2]

    def kernel(keep_ref, p, v, ds, k, context, query_grad):
        on = keep_ref[0] > 0
        for h in range(heads):
            at = slice(h * HD, (h + 1) * HD)
            context[:, at] = jnp.where(on, dot(p[h], v[:, at]), 0.0).astype(BF16)
            query_grad[:, at] = jnp.where(on, dot(ds[h], k[:, at]), 0.0).astype(BF16)

    return pl.pallas_call(
        kernel,
        in_specs=scalar() + whole(4),
        out_specs=whole(2),
        out_shape=[like((dec, local), BF16)] * 2,
        cost_estimate=cost(),
        compiler_params=params(),
    )(keep, low, values, dscores, keys)


def back_product_near(core, mine, key_weight, value_weight, packet, block, count):
    tokens = mine.shape[0]
    cols = key_weight.shape[1]
    width = 2 * block
    step = block // 2
    rows = tokens // count

    def kernel(core_ref, g, wk, wv, far, out, low, sems):
        c = core_ref[0]
        copies = []
        for i in range(width // step):
            at = (i // 2 * 2 + c) * 2 + i % 2
            total = dot(g[:, :cols], rows_of(wk, at, step), NT)
            total += dot(g[:, cols:], rows_of(wv, at, step), NT)
            for n in range(2):
                weight = far[n * width + i * step : n * width + (i + 1) * step, :]
                at = 2 * width + n * tokens
                total += dot(far[at : at + tokens, :], weight, NT)
            low[i] = total.reshape(count, rows, step).astype(BF16)
            copy = pltpu.make_async_copy(
                low.at[i], out.at[:, :, pl.ds(i * step, step)], sems.at[i]
            )
            copy.start()
            copies.append(copy)
        for copy in copies:
            copy.wait()

    return pl.pallas_call(
        kernel,
        in_specs=scalar() + whole(4),
        out_specs=pl.BlockSpec(memory_space=pltpu.HBM),
        out_shape=like((count, rows, width), BF16),
        scratch_shapes=[
            pltpu.VMEM((width // step, count, rows, step), BF16),
            pltpu.SemaphoreType.DMA((width // step,)),
        ],
        cost_estimate=cost(),
        compiler_params=params(),
    )(core, mine, key_weight, value_weight, packet)


def back_product(core, mine, others, key_weight, value_weight, packet, block, count):
    tokens = mine.shape[0]
    cols = key_weight.shape[1]
    width = 2 * block
    step = block // 2
    steps = width // step
    rows = tokens // count

    def kernel(core_ref, g, h, wk, wv, far, out, held, low, in_sems, out_sems):
        c = core_ref[0]
        loads = []
        for i in range(steps):
            at = pl.ds(pl.multiple_of(((i // 2 * 2 + c) * 2 + i % 2) * step, step), step)
            sources = [wk.at[at], wv.at[at]]
            sources += [far.at[pl.ds(n * width + i * step, step)] for n in range(2)]
            loads.append(
                [
                    pltpu.make_async_copy(source, held.at[i, n], in_sems.at[i, n])
                    for n, source in enumerate(sources)
                ]
            )
        for group in loads:
            for load in group:
                load.start()
        stores = []
        for i in range(steps):
            total = None
            for n, a in enumerate((g, g, h, h)):
                loads[i][n].wait()
                term = dot(a[:, n % 2 * cols : (n % 2 + 1) * cols], held[i, n], NT)
                total = term if total is None else total + term
            low[i] = total.reshape(count, rows, step).astype(BF16)
            store = pltpu.make_async_copy(
                low.at[i], out.at[:, :, pl.ds(i * step, step)], out_sems.at[i]
            )
            store.start()
            stores.append(store)
        for store in stores:
            store.wait()

    return pl.pallas_call(
        kernel,
        in_specs=scalar() + whole(2) + [pl.BlockSpec(memory_space=pl.ANY)] * 3,
        out_specs=pl.BlockSpec(memory_space=pl.ANY),
        out_shape=like((count, rows, width), BF16),
        scratch_shapes=[
            pltpu.VMEM((steps, 4, step, cols), BF16),
            pltpu.VMEM((steps, count, rows, step), BF16),
            pltpu.SemaphoreType.DMA((steps, 4)),
            pltpu.SemaphoreType.DMA((steps,)),
        ],
        cost_estimate=cost(),
        compiler_params=pltpu.CompilerParams(vmem_limit_bytes=VMEM_BACK),
    )(core, mine, others, key_weight, value_weight, packet)


def body(section_states, key_weight, value_weight, queries, cotangent):
    sections = lax.axis_size("pipe")
    replicas = lax.axis_size("dp")
    lanes = lax.axis_size("tensor")
    first = sections // 2
    count = sections - first
    root = first - 1
    section = lax.axis_index("pipe")
    replica = lax.axis_index("dp")
    lane = lax.axis_index("tensor")
    core = lane % 2
    chip = lane // 2
    chips = lanes // 2
    decoder = section >= first
    half = lanes // 2

    def place(s, d, t):
        return (s * replicas + d) * lanes + t

    everyone = [(k, d, t) for k in range(count) for d in range(replicas) for t in range(lanes)]

    def send(array, move):
        pairs = []
        for k, d, t in everyone:
            a, b, c = move(k, d, t)
            pairs.append((place(first + k, d, t), place(first + a, b, c)))
        return lax.ppermute(array, AXES, pairs)

    def swap_core(array):
        return send(array, lambda k, d, t: (k, d, t ^ 1))

    def swap_replica(array):
        return send(array, lambda k, d, t: (k, 1 - d, t))

    def beside(k, d, t):
        return place((k + count // 2) % count, d, t)

    def lend(array):
        pairs = [(place(first + k, d, t), beside(k, d, t)) for k, d, t in everyone]
        return lax.ppermute(array, AXES, pairs)

    def swap_replica_lent(array):
        pairs = [(beside(k, d, t), place(first + k, 1 - d, t)) for k, d, t in everyone]
        return lax.ppermute(array, AXES, pairs)

    groups = [list(range(first)), list(range(first, sections))]

    def exchange(array):
        return lax.all_to_all(array, "pipe", 0, 0, axis_index_groups=groups)

    def cross(k, d, t, n):
        over = 2 * (t % 2) + (n ^ (t % half) // 2)
        return (k, t // half, 2 * over + d)

    def cross_back(k, d, t, n):
        owner = (t // 2) ^ n
        return (k, owner // 2, half * d + 2 * (owner % 2) + t % 2)

    def in_order(mine, others):
        return jnp.where(core == 0, mine, others), jnp.where(core == 0, others, mine)

    piece = section_states[0, 0]
    key_weight, value_weight = key_weight[0], value_weight[0]
    tokens, block = piece.shape
    rows = tokens // count
    local = key_weight.shape[1]
    core_index = core.astype(jnp.int32).reshape(1)

    got = None
    for k in range(count):
        pairs = [
            (place(root, d, t), place(first + k, d, t))
            for d in range(replicas)
            for t in range(lanes)
        ]
        part = lax.ppermute(piece[k * rows : (k + 1) * rows], AXES, pairs)
        got = part if got is None else got + part
    both = jnp.concatenate(in_order(got, swap_core(got)), axis=1)
    held = [send(both, functools.partial(cross, n=n)) for n in range(2)]
    even = chip % 2 == 0
    chunk = jnp.concatenate(
        [jnp.where(even, held[0], held[1]), jnp.where(even, held[1], held[0])], axis=1
    )
    weights = [key_weight, value_weight]
    near = exchange(jnp.broadcast_to(chunk[None], (count,) + chunk.shape))
    far = swap_core(near)
    parts = [product_near(near, weight) for weight in weights]
    same = (core == replica).astype(jnp.int32).reshape(1)
    key_out, value_out, key_own, value_own = product_far(same, far, weights, parts, block)
    key_in = swap_replica(key_out)
    lent = lend(value_out)
    value_in = swap_replica_lent(lent)
    key_own = settle(key_own, lent)

    query, grad = queries[0, 0], cotangent[0, 0]
    keys, values, low, dscores, grads = attend(
        key_own, key_in, value_own, value_in, query, grad
    )
    grads_in = swap_replica(grads)
    keep = decoder.astype(jnp.int32).reshape(1)
    context, query_grad = attend_out(keep, low, values, dscores, keys)


    packet = swap_core(other_rows(core_index, *weights, grads, block))

    own_terms = exchange(
        back_product_near(core_index, grads, *weights, packet, block, count)
    )
    other_term = back_product(
        core_index, grads_in, swap_core(grads_in), *weights, packet, block, count
    )
    other_term, own_terms = lax.optimization_barrier((other_term, own_terms))
    own_total, other_total = (
        jnp.sum(terms.astype(F32), axis=0) for terms in (own_terms, exchange(other_term))
    )
    total = jnp.stack([own_total, other_total]).reshape(replicas, rows, 2, block)

    def owned(owner):
        one = lax.dynamic_index_in_dim(total, (owner // 2) ^ replica, 0, keepdims=False)
        return lax.dynamic_index_in_dim(one, owner % 2, 1, keepdims=False)

    summed = None
    for n in range(chips):
        part = send(owned(chip ^ n).astype(BF16), functools.partial(cross_back, n=n))
        part = part.astype(F32)
        summed = part if summed is None else summed + part
    summed = summed.astype(BF16)
    pairs = [
        (place(first + k, d, t), place(first + k - count // 2, d, t)) for k, d, t in everyone if k >= count // 2
    ]
    summed = jnp.concatenate([summed, lax.ppermute(summed, AXES, pairs)], axis=0)
    out = []
    for k in range(count // 2):
        pairs = [
            (place(first + k, d, t), place(root, d, t))
            for d in range(replicas)
            for t in range(lanes)
        ]
        out.append(lax.ppermute(summed, AXES, pairs))
    encoder_grad = jnp.concatenate([o[:rows] for o in out] + [o[rows:] for o in out], axis=0)
    encoder_grad = jnp.where(section == root, encoder_grad, jnp.zeros_like(encoder_grad))
    return context[None, None], query_grad[None, None], encoder_grad[None, None]


def solution(mesh):
    wide = P("pipe", "dp", None, "tensor")
    tall = P("pipe", "dp", "tensor")
    return jax.shard_map(
        body,
        mesh=mesh,
        in_specs=(wide, tall, tall, wide, wide),
        out_specs=(wide, wide, wide),
        check_vma=False,
    )
```
